32 devices in a mesh: ctx: 8 (over z, y), chan: 4 (over x, core).
Axes of the slice: x: 2, y: 2, z: 4, core: 2. Of those that a mesh axis runs over, the one named last changes fastest.
Arguments:
- query: bfloat16 [1, 1024, 8192], P(None, 'ctx', 'chan'), may hold values from -6 to 6
- key_in: bfloat16 [1, 1024, 8192], P(None, 'ctx', 'chan'), may hold values from -6 to 6
- value_in: bfloat16 [1, 1024, 8192], P(None, 'ctx', 'chan'), may hold values from -6 to 6
- cotangent: bfloat16 [1, 1024, 8192], P(None, 'ctx', 'chan'), may hold values from -6 to 6
- filters: float32 [512, 128], P('chan'), may hold values from -0.5 to 0.5
- norm_gain: float32 [8192], P('chan'), may hold values from 0.1 to 1.9
Outputs:
- normed: bfloat16 [1, 1024, 8192], P(None, 'ctx', 'chan')
- grad_query: bfloat16 [1, 1024, 8192], P(None, 'ctx', 'chan')
- grad_key: bfloat16 [1, 1024, 8192], P(None, 'ctx', 'chan')
- grad_value: bfloat16 [1, 1024, 8192], P(None, 'ctx', 'chan')
- grad_filters: float32 [512, 128], P('chan')
The draws below stay inside these ranges and needn't reach their ends.
All inputs are finite; a program needn't handle non-finite values.
Results may differ from the reference program's by a relative error of at most 0.0058.
Values may be sent and summed in bfloat16 or wider, within the bound.
A program may use at most 128 MiB of HBM per device.

```python
import jax
import jax.numpy as jnp
from jax import lax

D = 8192
GROUPS = 512
TAPS = 128
BATCH = 1
LENGTH = 1024


def block_scale(key, dims, cuts, low, largest):
    level, own = 1.0, jax.random.fold_in(key, 6)
    for dim, parts in cuts:
        heights = jnp.exp(jax.random.uniform(jax.random.fold_in(own, dim), (parts,), jnp.float32, low / len(cuts), largest / len(cuts)))
        level = level * jnp.repeat(heights, dims[dim] // parts).reshape([-1 if axis == dim else 1 for axis in range(len(dims))])
    return level


def centred(key, dims, scale, most, split=(), kind=jnp.bfloat16):
    level = block_scale(key, dims, split, -0.22, 0.18) if split else 1.0
    result = jax.random.normal(key, dims, jnp.float32) * scale * level
    return jnp.minimum(jnp.maximum(result, -most), most).astype(kind)


def setup_inputs(seed: int = 0) -> dict:
    key_list = jax.random.split(jax.random.key(seed), 7)
    return {
        "query": centred(key_list[0], (BATCH, LENGTH, D), 1.0, 6.0, ((1, 8), (2, 4))),
        "key_in": centred(key_list[1], (BATCH, LENGTH, D), 1.0, 6.0, ((1, 8), (2, 4))),
        "value_in": centred(key_list[2], (BATCH, LENGTH, D), 1.0, 6.0, ((1, 8), (2, 4))),
        "cotangent": centred(key_list[3], (BATCH, LENGTH, D), 1.0, 6.0, ((1, 8), (2, 4))),
        "filters": centred(key_list[4], (GROUPS, TAPS), TAPS ** -0.5, 0.5, ((0, 4),), jnp.float32),
        "norm_gain": jnp.clip(1.0 + 0.18 * jax.random.normal(key_list[5], (D,), jnp.float32), 0.1, 1.9),
    }


def toeplitz(taps):
    count, width = taps.shape
    zeros = jnp.zeros((count, width), taps.dtype)
    line = jnp.concatenate([zeros, jnp.flip(taps, 1), zeros], axis=1)
    tiled = jnp.tile(line, (1, width))
    tiled = tiled[:, :width * (3 * width - 1)].reshape(count, width, 3 * width - 1)
    return tiled[:, :, width - 1:3 * width - 1]

def lag_sums(pairs):
    count, width, double = pairs.shape
    flat = pairs.reshape(count, width * double)
    flat = jnp.concatenate([flat, jnp.zeros((count, width), pairs.dtype)], axis=1)
    skewed = flat.reshape(count, width, double + 1)
    totals = lax.optimization_barrier(jnp.sum(skewed, axis=1))
    return jnp.flip(totals[:, 1:width + 1], axis=1)

def reference(query, key_in, value_in, cotangent, filters, norm_gain):
    batch, length, width = query.shape
    groups, taps = filters.shape
    per = width // groups
    blocks_n = length // taps
    slabs = 8
    slab_groups = groups // slabs
    slab_width = slab_groups * per
    weights_all = toeplitz(filters.astype(jnp.bfloat16)).astype(jnp.float32)
    signal = (key_in.astype(jnp.float32) * value_in.astype(jnp.float32)).astype(jnp.bfloat16)
    windows = []
    mixed_parts = []
    for slab in range(slabs):
        lo = slab * slab_width
        weights = weights_all[slab * slab_groups:(slab + 1) * slab_groups]
        blocks = signal[:, :, lo:lo + slab_width].reshape(batch, blocks_n, taps, slab_groups, per)
        before = jnp.concatenate([jnp.zeros_like(blocks[:, :1]), blocks[:, :-1]], axis=1)
        window = jnp.concatenate([before, blocks], axis=2).reshape(batch * blocks_n, 2 * taps, slab_groups, per)
        windows.append(window)
        part = jnp.einsum('gts,bsgc->btgc', weights, window.astype(jnp.float32), precision=lax.Precision.HIGHEST)
        mixed_parts.append(part.reshape(batch, length, slab_width))
    mixed = jnp.concatenate(mixed_parts, axis=2)
    lifted = query.astype(jnp.float32) * mixed
    scaled = norm_gain * cotangent.astype(jnp.float32)
    power = lax.optimization_barrier(jnp.sum(lifted * lifted, axis=-1))
    inner = lax.optimization_barrier(jnp.sum(scaled * lifted, axis=-1))[..., None]
    recip = lax.rsqrt(power / D + 1e-06)[..., None]
    normed = (lifted * recip * norm_gain).astype(jnp.bfloat16)
    grad_mix = recip * scaled - lifted * recip ** 3 * inner / D
    grad_query = (grad_mix * mixed).astype(jnp.bfloat16)
    grad_conv = (grad_mix * query.astype(jnp.float32)).astype(jnp.bfloat16)
    extended = jnp.concatenate([grad_conv, jnp.zeros((batch, taps, width), jnp.bfloat16)], axis=1)
    grad_parts = []
    filter_parts = []
    for slab in range(slabs):
        lo = slab * slab_width
        weights = weights_all[slab * slab_groups:(slab + 1) * slab_groups]
        gathered = extended[:, :, lo:lo + slab_width].reshape(batch * (blocks_n + 1), taps, slab_groups, per)
        back = jnp.einsum('gts,btgc->bsgc', weights, gathered.astype(jnp.float32), precision=lax.Precision.HIGHEST)
        back = back.reshape(batch, blocks_n + 1, 2 * taps, slab_width)
        grad_parts.append((back[:, :blocks_n, taps:] + back[:, 1:, :taps]).reshape(batch, length, slab_width))
        own = grad_conv[:, :, lo:lo + slab_width].reshape(batch * blocks_n, taps, slab_groups, per)
        pairs = jnp.einsum('btgc,bsgc->gts', own.astype(jnp.float32), windows[slab].astype(jnp.float32), precision=lax.Precision.HIGHEST)
        filter_parts.append(lag_sums(pairs))
    grad_signal = jnp.concatenate(grad_parts, axis=2)
    grad_key = (grad_signal * value_in.astype(jnp.float32)).astype(jnp.bfloat16)
    grad_value = (grad_signal * key_in.astype(jnp.float32)).astype(jnp.bfloat16)
    grad_filters = jnp.concatenate(filter_parts, axis=0)
    return (normed, grad_query, grad_key, grad_value, grad_filters)
```

```python
import functools

import jax
import jax.numpy as jnp
from jax import lax
from jax.experimental import pallas as pl
from jax.experimental.pallas import tpu as pltpu
from jax.sharding import PartitionSpec as P

D = 8192
LANES = 256
MESH = pl.DeviceIdType.MESH


def iota(shape, axis):
    return lax.broadcasted_iota(jnp.int32, shape, axis)


def kernel(
    n_ctx, n_chan, members, own_sum,
    q_ref, k_ref, v_ref, ct_ref, f_ref, gain_ref,
    normed_ref, gq_ref, gk_ref, gv_ref, gf_ref,
    win, gwin, srev, fwd, bwd, frev, taps32, mixed, power, inner, stats, part, land,
    sig_send, sig_recv, gc_send, gc_recv, st_send, st_recv, rs_send, rs_recv, ag_send, ag_recv,
):
    f32, bf16 = jnp.float32, jnp.bfloat16
    rows = q_ref.shape[0]
    nb = q_ref.shape[1] // LANES
    groups = f_ref.shape[0]
    per = LANES // members
    me, chan = lax.axis_index("ctx"), lax.axis_index("chan")
    last = n_ctx - 1

    barrier = pltpu.get_barrier_semaphore()
    chan_peers = [lax.rem(chan + d, n_chan) for d in range(1, n_chan)]
    for peer in chan_peers:
        pl.semaphore_signal(barrier, inc=1, device_id=(me, peer), device_id_type=MESH)
    if own_sum:
        ctx_peers = [lax.rem(me + d, n_ctx) for d in range(1, n_ctx)]
        for peer in ctx_peers:
            pl.semaphore_signal(barrier, inc=1, device_id=(peer, chan), device_id_type=MESH)
        pl.semaphore_wait(barrier, n_chan - 1 + n_ctx - 1)
    else:
        for step in (1, n_ctx - 1):
            pl.semaphore_signal(
                barrier, inc=1, device_id=(lax.rem(me + step, n_ctx), chan), device_id_type=MESH
            )
        pl.semaphore_wait(barrier, n_chan - 1 + 2)

    def lanes(c):
        return pl.ds(pl.multiple_of(c * LANES, LANES), LANES)

    def signal_copy(c):
        return pltpu.make_async_remote_copy(
            src_ref=win.at[c, pl.ds(rows, rows), :],
            dst_ref=win.at[c, pl.ds(0, rows), :],
            send_sem=sig_send.at[c], recv_sem=sig_recv.at[c],
            device_id=(jnp.minimum(me + 1, last), chan), device_id_type=MESH,
        )

    def conv_copy(c):
        return pltpu.make_async_remote_copy(
            src_ref=gwin.at[c, pl.ds(0, rows), :],
            dst_ref=gwin.at[c, pl.ds(rows, rows), :],
            send_sem=gc_send.at[c], recv_sem=gc_recv.at[c],
            device_id=(jnp.maximum(me - 1, 0), chan), device_id_type=MESH,
        )

    @pl.loop(0, nb)
    def _(c):
        key = k_ref[:, lanes(c)].astype(f32)
        win[c, rows:, :] = (key * v_ref[:, lanes(c)].astype(f32)).astype(bf16)

        @pl.when(me < last)
        def _():
            signal_copy(c).start()

        @pl.when(me == 0)
        def _():
            win[c, :rows, :] = jnp.zeros((rows, LANES), bf16)

        @pl.when(me == last)
        def _():
            gwin[c, rows:, :] = jnp.zeros((rows, LANES), bf16)

    row, col = iota((rows, rows), 0), iota((rows, rows), 1)
    taps_b = f_ref[...].astype(bf16)
    taps32[...] = taps_b.astype(f32)
    negate = (lax.rem(row + col, rows) == 0).astype(f32).astype(bf16)
    frev[...] = jnp.dot(taps_b, negate, preferred_element_type=f32)

    @pl.loop(0, groups)
    def _(g):
        at = pl.ds(pl.multiple_of(g * rows, rows), rows)
        turned = jnp.broadcast_to(frev[pl.ds(g, 1), :], (rows, rows))
        turned = pltpu.roll(turned, 0, 1, stride=1, stride_axis=0)
        fwd[at, :rows] = jnp.where(col > row, turned, 0.0).astype(bf16)
        fwd[at, rows:] = jnp.where(col <= row, turned, 0.0).astype(bf16)
        plain = jnp.broadcast_to(taps32[pl.ds(g, 1), :], (rows, rows))
        plain = pltpu.roll(plain, 0, 1, stride=1, stride_axis=0)
        bwd[at, :rows] = jnp.where(col >= row, plain, 0.0).astype(bf16)
        bwd[at, rows:] = jnp.where(col < row, plain, 0.0).astype(bf16)

    lane_group = iota((rows, LANES), 1) // members
    flip = (row + col == rows - 1).astype(f32).astype(bf16)
    power[...] = jnp.zeros_like(power)
    inner[...] = jnp.zeros_like(inner)

    def filtered(matrices, window, c):
        total = jnp.zeros((rows, LANES), f32)
        for k in range(per):
            at = pl.ds(pl.multiple_of((c * per + k) * rows, rows), rows)
            out = jnp.dot(matrices[at, :], window, preferred_element_type=f32)
            total = jnp.where(lane_group == k, out, total)
        return total

    @pl.loop(0, nb)
    def _(c):
        @pl.when(me > 0)
        def _():
            signal_copy(c).wait_recv()

        window = win[c]
        mix = filtered(fwd, window, c)
        mixed[c] = mix
        lifted = q_ref[:, lanes(c)].astype(f32) * mix
        scaled = gain_ref[:, lanes(c)] * ct_ref[:, lanes(c)].astype(f32)
        square, cross = lifted * lifted, scaled * lifted
        half = LANES // 2
        power[...] += square[:, :half] + square[:, half:]
        inner[...] += cross[:, :half] + cross[:, half:]
        srev[c, :rows, :] = jnp.dot(flip, window[rows:], preferred_element_type=f32).astype(bf16)
        srev[c, rows:, :] = jnp.dot(flip, window[:rows], preferred_element_type=f32).astype(bf16)

    stats[chan, 0:1, :] = jnp.sum(power[...].T, axis=0, keepdims=True)
    stats[chan, 1:2, :] = jnp.sum(inner[...].T, axis=0, keepdims=True)
    stats[chan, 2:, :] = jnp.zeros((6, rows), f32)

    def stat_copy(d, slot):
        return pltpu.make_async_remote_copy(
            src_ref=stats.at[slot], dst_ref=stats.at[slot],
            send_sem=st_send.at[d], recv_sem=st_recv.at[d],
            device_id=(me, chan_peers[d]), device_id_type=MESH,
        )

    for d in range(n_chan - 1):
        stat_copy(d, chan).start()
    for d in range(n_chan - 1):
        stat_copy(d, lax.rem(chan + n_chan - d - 1, n_chan)).wait_recv()
    sums = jnp.sum(stats[...], axis=0)
    recip_row = lax.rsqrt(sums[0:1] / D + 1e-06)
    slope_row = recip_row * recip_row * recip_row * sums[1:2] / D
    recip = jnp.broadcast_to(recip_row, (rows, rows)).T
    slope = jnp.broadcast_to(slope_row, (rows, rows)).T
    power[...] = recip
    inner[...] = slope

    @pl.loop(0, nb)
    def _(c):
        recip = jnp.concatenate([power[...]] * (LANES // rows), axis=1)
        slope = jnp.concatenate([inner[...]] * (LANES // rows), axis=1)
        mix = mixed[c]
        query = q_ref[:, lanes(c)].astype(f32)
        gain = gain_ref[:, lanes(c)]
        lifted = query * mix
        scaled = gain * ct_ref[:, lanes(c)].astype(f32)
        grad_mix = recip * scaled - lifted * slope
        gwin[c, :rows, :] = (grad_mix * query).astype(bf16)

        @pl.when(me > 0)
        def _():
            conv_copy(c).start()

        normed_ref[:, lanes(c)] = (lifted * recip * gain).astype(bf16)
        gq_ref[:, lanes(c)] = (grad_mix * mix).astype(bf16)

    @pl.loop(0, nb)
    def _(c):
        conv = gwin[c, :rows, :].astype(f32)
        turned = srev[c]
        for k in range(per):
            masked = jnp.where(lane_group == k, conv, 0.0).astype(bf16)
            pairs = lax.dot_general(
                masked, turned, (((1,), (1,)), ((), ())), preferred_element_type=f32
            )
            both = jnp.where(row + col >= rows - 1, pairs[:, :rows], pairs[:, rows:])
            both = pltpu.roll(both, 1, 1, stride=1, stride_axis=0)
            part[pl.ds(c * per + k, 1), :] = jnp.sum(both, axis=0, keepdims=True)

    share = groups // n_ctx

    def scatter_copy(d):
        peer = ctx_peers[d]
        return pltpu.make_async_remote_copy(
            src_ref=part.at[pl.ds(pl.multiple_of(peer * share, share), share), :],
            dst_ref=land.at[d],
            send_sem=rs_send.at[d], recv_sem=rs_recv.at[d],
            device_id=(peer, chan), device_id_type=MESH,
        )

    def gather_copy(d, owner):
        at = pl.ds(pl.multiple_of(owner * share, share), share)
        return pltpu.make_async_remote_copy(
            src_ref=gf_ref.at[at, :], dst_ref=gf_ref.at[at, :],
            send_sem=ag_send.at[d], recv_sem=ag_recv.at[d],
            device_id=(ctx_peers[d], chan), device_id_type=MESH,
        )

    if own_sum:
        for d in range(n_ctx - 1):
            scatter_copy(d).start()
    else:
        gf_ref[...] = part[...]

    def back(c):
        @pl.when(me < last)
        def _():
            conv_copy(c).wait_recv()

        grad_signal = filtered(bwd, gwin[c], c)
        gk_ref[:, lanes(c)] = (grad_signal * v_ref[:, lanes(c)].astype(f32)).astype(bf16)
        gv_ref[:, lanes(c)] = (grad_signal * k_ref[:, lanes(c)].astype(f32)).astype(bf16)

    pl.loop(0, nb // 2)(back)
    if own_sum:
        for d in range(n_ctx - 1):
            scatter_copy(d).wait_recv()
        at = pl.ds(pl.multiple_of(me * share, share), share)
        gf_ref[at, :] = part[at, :] + jnp.sum(land[...], axis=0)
        for d in range(n_ctx - 1):
            gather_copy(d, me).start()
    pl.loop(nb // 2, nb)(back)

    if own_sum:
        for d in range(n_ctx - 1):
            gather_copy(d, lax.rem(me + n_ctx - d - 1, n_ctx)).wait_recv()
            gather_copy(d, me).wait_send()
            scatter_copy(d).wait_send()
    for d in range(n_chan - 1):
        stat_copy(d, chan).wait_send()

    @pl.loop(0, nb)
    def _(c):
        @pl.when(me < last)
        def _():
            signal_copy(c).wait_send()

        @pl.when(me > 0)
        def _():
            conv_copy(c).wait_send()


def body(n_ctx, n_chan, query, key_in, value_in, cotangent, filters, norm_gain):
    batch, rows, width = query.shape
    groups, taps = filters.shape
    assert batch == 1 and rows == taps
    members = width // groups
    nb = width // LANES
    own_sum = groups % (8 * n_ctx) == 0
    share = max(groups // n_ctx, 8)
    f32, bf16 = jnp.float32, jnp.bfloat16
    flat = jax.ShapeDtypeStruct((rows, width), bf16)
    vmem = pl.BlockSpec(memory_space=pltpu.VMEM)
    dma = pltpu.SemaphoreType.DMA
    outs = pl.pallas_call(
        functools.partial(kernel, n_ctx, n_chan, members, own_sum),
        out_shape=(flat, flat, flat, flat, jax.ShapeDtypeStruct((groups, taps), f32)),
        in_specs=[vmem] * 6,
        out_specs=(vmem,) * 5,
        scratch_shapes=[
            pltpu.VMEM((nb, 2 * rows, LANES), bf16),
            pltpu.VMEM((nb, 2 * rows, LANES), bf16),
            pltpu.VMEM((nb, 2 * rows, LANES), bf16),
            pltpu.VMEM((groups * rows, 2 * rows), bf16),
            pltpu.VMEM((groups * rows, 2 * rows), bf16),
            pltpu.VMEM((groups, taps), f32),
            pltpu.VMEM((groups, taps), f32),
            pltpu.VMEM((nb, rows, LANES), f32),
            pltpu.VMEM((rows, rows), f32),
            pltpu.VMEM((rows, rows), f32),
            pltpu.VMEM((n_chan, 8, rows), f32),
            pltpu.VMEM((groups, taps), f32),
            pltpu.VMEM((n_ctx - 1, share, taps), f32),
            dma((nb,)), dma((nb,)), dma((nb,)), dma((nb,)),
            dma((n_chan - 1,)), dma((n_chan - 1,)),
            dma((n_ctx - 1,)), dma((n_ctx - 1,)), dma((n_ctx - 1,)), dma((n_ctx - 1,)),
        ],
        compiler_params=pltpu.CompilerParams(
            collective_id=0, has_side_effects=True, vmem_limit_bytes=48 << 20
        ),
    )(
        *(x.reshape(rows, width) for x in (query, key_in, value_in, cotangent)),
        filters,
        norm_gain.reshape(1, width),
    )
    grad_filters = outs[4] if own_sum else lax.psum(outs[4], "ctx")
    return tuple(x.reshape(1, rows, width) for x in outs[:4]) + (grad_filters,)


def solution(mesh):
    spread = P(None, "ctx", "chan")
    return jax.shard_map(
        functools.partial(body, mesh.shape["ctx"], mesh.shape["chan"]),
        mesh=mesh,
        in_specs=(spread,) * 4 + (P("chan", None), P("chan")),
        out_specs=(spread,) * 4 + (P("chan", None),),
        check_vma=False,
    )
```

```python
import functools

import jax
import jax.numpy as jnp
from jax import lax
from jax.experimental import pallas as pl
from jax.experimental.pallas import tpu as pltpu
from jax.sharding import PartitionSpec as P

D = 8192
LANES = 256
MESH = pl.DeviceIdType.MESH


def iota(shape, axis):
    return lax.broadcasted_iota(jnp.int32, shape, axis)


def kernel(
    n_ctx, n_chan, members, own_sum,
    q_hbm, k_hbm, v_hbm, ct_hbm, f_hbm, gain_hbm,
    normed_hbm, gq_hbm, gk_hbm, gv_hbm, gf_hbm,
    normed_ref, gq_ref, gk_ref, gv_ref, gf_ref, out_sem, gk_sem, gv_sem,
    q_ref, k_ref, v_ref, ct_ref, f_ref, gain_ref, in_sem,
    win, gwin, srev, own, fwd, frev, mixed, power, inner, stats, part, land,
    sig_send, sig_recv, gc_send, gc_recv, st_send, st_recv, rs_send, rs_recv, ag_send, ag_recv,
):
    f32, bf16 = jnp.float32, jnp.bfloat16
    rows = q_ref.shape[0]
    nb = q_ref.shape[1] // LANES
    groups = f_ref.shape[0]
    per = LANES // members
    me, chan = lax.axis_index("ctx"), lax.axis_index("chan")
    last = n_ctx - 1

    loads = [
        pltpu.make_async_copy(src, dst, in_sem.at[n])
        for n, (src, dst) in enumerate([
            (k_hbm, k_ref), (v_hbm, v_ref), (f_hbm, f_ref),
            (q_hbm, q_ref), (ct_hbm, ct_ref), (gain_hbm, gain_ref),
        ])
    ]
    for load in loads:
        load.start()
    barrier = pltpu.get_barrier_semaphore()
    chan_peers = [lax.rem(chan + d, n_chan) for d in range(1, n_chan)]
    near = range(1, n_ctx) if own_sum else sorted({1, n_ctx - 1})
    for peer in chan_peers:
        pl.semaphore_signal(barrier, inc=1, device_id=(me, peer), device_id_type=MESH)
    for d in near:
        pl.semaphore_signal(
            barrier, inc=1, device_id=(lax.rem(me + d, n_ctx), chan), device_id_type=MESH
        )

    def ctx_peer(d):
        return lax.rem(me + d + 1, n_ctx)

    def lanes(c):
        return pl.ds(pl.multiple_of(c * LANES, LANES), LANES)

    def signal_copy(c):
        return pltpu.make_async_remote_copy(
            src_ref=win.at[c, pl.ds(rows, rows), :],
            dst_ref=win.at[c, pl.ds(0, rows), :],
            send_sem=sig_send.at[c], recv_sem=sig_recv.at[c],
            device_id=(jnp.minimum(me + 1, last), chan), device_id_type=MESH,
        )

    def conv_copy(c):
        return pltpu.make_async_remote_copy(
            src_ref=gwin.at[c, pl.ds(rows, rows), :],
            dst_ref=gwin.at[c, pl.ds(0, rows), :],
            send_sem=gc_send.at[c], recv_sem=gc_recv.at[c],
            device_id=(jnp.maximum(me - 1, 0), chan), device_id_type=MESH,
        )

    loads[0].wait()
    loads[1].wait()

    @pl.loop(0, nb)
    def _(c):
        key = k_ref[:, lanes(c)].astype(f32)
        win[c, rows:, :] = (key * v_ref[:, lanes(c)].astype(f32)).astype(bf16)

        @pl.when(me == 0)
        def _():
            win[c, :rows, :] = jnp.zeros((rows, LANES), bf16)

        @pl.when(me == last)
        def _():
            gwin[c, :rows, :] = jnp.zeros((rows, LANES), bf16)

    pl.semaphore_wait(barrier, n_chan - 1 + len(near))

    @pl.when(me < last)
    def _():
        @pl.loop(0, nb)
        def _(c):
            signal_copy(c).start()

    row, col = iota((rows, rows), 0), iota((rows, rows), 1)
    loads[2].wait()
    taps_b = f_ref[...].astype(bf16)
    negate = (lax.rem(row + col, rows) == 0).astype(f32).astype(bf16)
    frev[...] = jnp.dot(taps_b, negate, preferred_element_type=f32)

    @pl.loop(0, groups)
    def _(g):
        at = pl.ds(pl.multiple_of(g * rows, rows), rows)
        turned = jnp.broadcast_to(frev[pl.ds(g, 1), :], (rows, rows))
        turned = pltpu.roll(turned, 0, 1, stride=1, stride_axis=0)
        fwd[at, :rows] = jnp.where(col > row, turned, 0.0).astype(bf16)
        fwd[at, rows:] = jnp.where(col <= row, turned, 0.0).astype(bf16)

    lane_group = iota((rows, LANES), 1) // members
    flip = (row + col == rows - 1).astype(f32).astype(bf16)
    power[...] = jnp.zeros_like(power)
    inner[...] = jnp.zeros_like(inner)
    for load in loads[3:]:
        load.wait()

    def filtered(window, c):
        total = jnp.zeros((rows, LANES), f32)
        for k in range(per):
            at = pl.ds(pl.multiple_of((c * per + k) * rows, rows), rows)
            out = jnp.dot(fwd[at, :], window, preferred_element_type=f32)
            total = jnp.where(lane_group == k, out, total)
        return total

    @pl.loop(0, nb)
    def _(c):
        @pl.when(me > 0)
        def _():
            signal_copy(c).wait_recv()

        window = win[c]
        mix = filtered(window, c)
        mixed[c] = mix
        lifted = q_ref[:, lanes(c)].astype(f32) * mix
        scaled = gain_ref[:, lanes(c)] * ct_ref[:, lanes(c)].astype(f32)
        square, cross = lifted * lifted, scaled * lifted
        half = LANES // 2
        power[...] += square[:, :half] + square[:, half:]
        inner[...] += cross[:, :half] + cross[:, half:]
        srev[c, :rows, :] = jnp.dot(flip, window[rows:], preferred_element_type=f32).astype(bf16)
        srev[c, rows:, :] = jnp.dot(flip, window[:rows], preferred_element_type=f32).astype(bf16)

    stats[chan, 0:1, :] = jnp.sum(power[...].T, axis=0, keepdims=True)
    stats[chan, 1:2, :] = jnp.sum(inner[...].T, axis=0, keepdims=True)
    stats[chan, 2:, :] = jnp.zeros((6, rows), f32)

    def stat_copy(d, slot):
        return pltpu.make_async_remote_copy(
            src_ref=stats.at[slot], dst_ref=stats.at[slot],
            send_sem=st_send.at[d], recv_sem=st_recv.at[d],
            device_id=(me, chan_peers[d]), device_id_type=MESH,
        )

    for d in range(n_chan - 1):
        stat_copy(d, chan).start()
    for d in range(n_chan - 1):
        stat_copy(d, lax.rem(chan + n_chan - d - 1, n_chan)).wait_recv()
    sums = jnp.sum(stats[...], axis=0)
    recip_row = lax.rsqrt(sums[0:1] / D + 1e-06)
    slope_row = recip_row * recip_row * recip_row * sums[1:2] / D
    recip = jnp.broadcast_to(recip_row, (rows, rows)).T
    slope = jnp.broadcast_to(slope_row, (rows, rows)).T
    power[...] = recip
    inner[...] = slope

    @pl.loop(0, nb)
    def _(c):
        recip = jnp.concatenate([power[...]] * (LANES // rows), axis=1)
        slope = jnp.concatenate([inner[...]] * (LANES // rows), axis=1)
        mix = mixed[c]
        query = q_ref[:, lanes(c)].astype(f32)
        gain = gain_ref[:, lanes(c)]
        lifted = query * mix
        scaled = gain * ct_ref[:, lanes(c)].astype(f32)
        grad_mix = recip * scaled - lifted * slope
        conv = (grad_mix * query).astype(bf16)
        own[c] = conv
        gwin[c, rows:, :] = jnp.dot(flip, conv, preferred_element_type=f32).astype(bf16)

        @pl.when(me > 0)
        def _():
            conv_copy(c).start()

        normed_ref[:, lanes(c)] = (lifted * recip * gain).astype(bf16)
        gq_ref[:, lanes(c)] = (grad_mix * mix).astype(bf16)

    saves = [
        pltpu.make_async_copy(src, dst, out_sem.at[n])
        for n, (src, dst) in enumerate(
            [(normed_ref, normed_hbm), (gq_ref, gq_hbm), (gf_ref, gf_hbm)]
        )
    ]
    saves[0].start()
    saves[1].start()

    def key_save(c):
        return pltpu.make_async_copy(
            gk_ref.at[:, lanes(c)], gk_hbm.at[:, lanes(c)], gk_sem.at[c]
        )

    def value_save(c):
        return pltpu.make_async_copy(
            gv_ref.at[:, lanes(c)], gv_hbm.at[:, lanes(c)], gv_sem.at[c]
        )

    def scatter_copy(d):
        peer = ctx_peer(d)
        return pltpu.make_async_remote_copy(
            src_ref=part.at[pl.ds(pl.multiple_of(peer * per, per), per), :],
            dst_ref=land.at[d],
            send_sem=rs_send.at[d], recv_sem=rs_recv.at[d],
            device_id=(peer, chan), device_id_type=MESH,
        )

    def gather_copy(d, owner):
        at = pl.ds(pl.multiple_of(owner * per, per), per)
        return pltpu.make_async_remote_copy(
            src_ref=gf_ref.at[at, :], dst_ref=gf_ref.at[at, :],
            send_sem=ag_send.at[d], recv_sem=ag_recv.at[d],
            device_id=(ctx_peer(d), chan), device_id_type=MESH,
        )

    @pl.loop(0, nb)
    def _(i):
        c = lax.rem(me + 1 + i, nb) if own_sum else i
        conv = own[c].astype(f32)
        turned = srev[c]
        for k in range(per):
            masked = jnp.where(lane_group == k, conv, 0.0).astype(bf16)
            pairs = lax.dot_general(
                masked, turned, (((1,), (1,)), ((), ())), preferred_element_type=f32
            )
            both = jnp.where(row + col >= rows - 1, pairs[:, :rows], pairs[:, rows:])
            both = pltpu.roll(both, 1, 1, stride=1, stride_axis=0)
            part[pl.ds(c * per + k, 1), :] = jnp.sum(both, axis=0, keepdims=True)
        if own_sum:
            @pl.when(i < nb - 1)
            def _():
                scatter_copy(i).start()

    def back(c):
        @pl.when(me < last)
        def _():
            conv_copy(c).wait_recv()

        turned = filtered(gwin[c], c)
        high = turned.astype(bf16)
        low = (turned - high.astype(f32)).astype(bf16)
        grad_signal = jnp.dot(
            jnp.concatenate([flip, flip], axis=1),
            jnp.concatenate([high, low], axis=0),
            preferred_element_type=f32,
        )
        gk_ref[:, lanes(c)] = (grad_signal * v_ref[:, lanes(c)].astype(f32)).astype(bf16)
        gv_ref[:, lanes(c)] = (grad_signal * k_ref[:, lanes(c)].astype(f32)).astype(bf16)
        key_save(c).start()
        value_save(c).start()

    pl.loop(0, nb // 2)(back)
    if own_sum:
        for d in range(n_ctx - 1):
            scatter_copy(d).wait_recv()
        at = pl.ds(pl.multiple_of(me * per, per), per)
        gf_ref[at, :] = part[at, :] + jnp.sum(land[...], axis=0)
        for d in range(n_ctx - 1):
            gather_copy(d, me).start()
    else:
        gf_ref[...] = part[...]
    pl.loop(nb // 2, nb)(back)

    if own_sum:
        for d in range(n_ctx - 1):
            gather_copy(d, lax.rem(me + n_ctx - d - 1, n_ctx)).wait_recv()
        saves[2].start()
        for d in range(n_ctx - 1):
            gather_copy(d, me).wait_send()
            scatter_copy(d).wait_send()
    else:
        saves[2].start()
    for d in range(n_chan - 1):
        stat_copy(d, chan).wait_send()

    @pl.loop(0, nb)
    def _(c):
        @pl.when(me < last)
        def _():
            signal_copy(c).wait_send()

        @pl.when(me > 0)
        def _():
            conv_copy(c).wait_send()

        key_save(c).wait()
        value_save(c).wait()

    for save in saves:
        save.wait()


def store(*refs):
    held, taken, given = refs[10:15], refs[15], refs[16]
    reads = [pltpu.make_async_copy(refs[n], held[n], taken.at[n]) for n in range(5)]
    writes = [pltpu.make_async_copy(held[n], refs[5 + n], given.at[n]) for n in range(5)]
    for copy in reads:
        copy.start()
    for read, write in zip(reads, writes):
        read.wait()
        write.start()
    for copy in writes:
        copy.wait()


def body(n_ctx, n_chan, query, key_in, value_in, cotangent, filters, norm_gain):
    batch, rows, width = query.shape
    groups, taps = filters.shape
    assert batch == 1 and rows == taps
    members = width // groups
    nb = width // LANES
    own_sum = nb == n_ctx
    f32, bf16 = jnp.float32, jnp.bfloat16
    flat = jax.ShapeDtypeStruct((rows, width), bf16)
    hbm = pl.BlockSpec(memory_space=pltpu.HBM)
    dma = pltpu.SemaphoreType.DMA
    outs = pl.pallas_call(
        functools.partial(kernel, n_ctx, n_chan, members, own_sum),
        out_shape=(flat, flat, flat, flat, jax.ShapeDtypeStruct((groups, taps), f32)),
        in_specs=[hbm] * 6,
        out_specs=(hbm,) * 5,
        scratch_shapes=[
            *[pltpu.VMEM((rows, width), bf16)] * 4,
            pltpu.VMEM((groups, taps), f32),
            dma((3,)), dma((nb,)), dma((nb,)),
            *[pltpu.VMEM((rows, width), bf16)] * 4,
            pltpu.VMEM((groups, taps), f32),
            pltpu.VMEM((1, width), f32),
            dma((6,)),
            pltpu.VMEM((nb, 2 * rows, LANES), bf16),
            pltpu.VMEM((nb, 2 * rows, LANES), bf16),
            pltpu.VMEM((nb, 2 * rows, LANES), bf16),
            pltpu.VMEM((nb, rows, LANES), bf16),
            pltpu.VMEM((groups * rows, 2 * rows), bf16),
            pltpu.VMEM((groups, taps), f32),
            pltpu.VMEM((nb, rows, LANES), f32),
            pltpu.VMEM((rows, rows), f32),
            pltpu.VMEM((rows, rows), f32),
            pltpu.VMEM((n_chan, 8, rows), f32),
            pltpu.VMEM((groups, taps), f32),
            pltpu.VMEM((n_ctx - 1, LANES // members, taps), f32),
            dma((nb,)), dma((nb,)), dma((nb,)), dma((nb,)),
            dma((n_chan - 1,)), dma((n_chan - 1,)),
            dma((n_ctx - 1,)), dma((n_ctx - 1,)), dma((n_ctx - 1,)), dma((n_ctx - 1,)),
        ],
        compiler_params=pltpu.CompilerParams(
            collective_id=0, has_side_effects=True, vmem_limit_bytes=60 << 20
        ),
    )(
        *(x.reshape(rows, width) for x in (query, key_in, value_in, cotangent)),
        filters,
        norm_gain.reshape(1, width),
    )
    outs = pl.pallas_call(
        store,
        out_shape=tuple(jax.ShapeDtypeStruct(x.shape, x.dtype) for x in outs),
        in_specs=[hbm] * 5,
        out_specs=(hbm,) * 5,
        scratch_shapes=[*[pltpu.VMEM(x.shape, x.dtype) for x in outs], dma((5,)), dma((5,))],
        compiler_params=pltpu.CompilerParams(vmem_limit_bytes=60 << 20),
    )(*outs)
    grad_filters = outs[4] if own_sum else lax.psum(outs[4], "ctx")
    return tuple(x.reshape(1, rows, width) for x in outs[:4]) + (grad_filters,)


def solution(mesh):
    spread = P(None, "ctx", "chan")
    return jax.shard_map(
        functools.partial(body, mesh.shape["ctx"], mesh.shape["chan"]),
        mesh=mesh,
        in_specs=(spread,) * 4 + (P("chan", None), P("chan")),
        out_specs=(spread,) * 4 + (P("chan", None),),
        check_vma=False,
    )
```

```python
import functools

import jax
import jax.numpy as jnp
from jax import lax
from jax.experimental import pallas as pl
from jax.experimental.pallas import tpu as pltpu
from jax.sharding import PartitionSpec as P

D = 8192
LANES = 256
MESH = pl.DeviceIdType.MESH


def iota(shape, axis):
    return lax.broadcasted_iota(jnp.int32, shape, axis)


def kernel(
    n_ctx, n_chan, members, own_sum,
    q_hbm, k_hbm, v_hbm, ct_hbm, f_hbm, gain_hbm,
    normed_hbm, gq_hbm, gk_hbm, gv_hbm, gf_hbm,
    normed_ref, gq_ref, gk_ref, gv_ref, gf_ref, out_sem, gk_sem, gv_sem,
    q_ref, k_ref, v_ref, ct_ref, f_ref, gain_ref, in_sem,
    win, gwin, srev, own, fwd, frev, mixed, power, inner, stats, part, land,
    sig_send, sig_recv, gc_send, gc_recv, st_send, st_recv, rs_send, rs_recv, ag_send, ag_recv,
):
    f32, bf16 = jnp.float32, jnp.bfloat16
    rows = q_ref.shape[0]
    nb = q_ref.shape[1] // LANES
    groups = f_ref.shape[0]
    per = LANES // members
    me, chan = lax.axis_index("ctx"), lax.axis_index("chan")
    last = n_ctx - 1

    loads = [
        pltpu.make_async_copy(src, dst, in_sem.at[n])
        for n, (src, dst) in enumerate([
            (k_hbm, k_ref), (v_hbm, v_ref), (f_hbm, f_ref),
            (q_hbm, q_ref), (ct_hbm, ct_ref), (gain_hbm, gain_ref),
        ])
    ]
    for load in loads:
        load.start()
    barrier = pltpu.get_barrier_semaphore()
    chan_peers = [lax.rem(chan + d, n_chan) for d in range(1, n_chan)]
    near = range(1, n_ctx) if own_sum else sorted({1, n_ctx - 1})
    for peer in chan_peers:
        pl.semaphore_signal(barrier, inc=1, device_id=(me, peer), device_id_type=MESH)
    for d in near:
        pl.semaphore_signal(
            barrier, inc=1, device_id=(lax.rem(me + d, n_ctx), chan), device_id_type=MESH
        )

    def ctx_peer(d):
        return lax.rem(me + d + 1, n_ctx)

    def lanes(c):
        return pl.ds(pl.multiple_of(c * LANES, LANES), LANES)

    def signal_copy(c):
        return pltpu.make_async_remote_copy(
            src_ref=win.at[c, pl.ds(rows, rows), :],
            dst_ref=win.at[c, pl.ds(0, rows), :],
            send_sem=sig_send.at[c], recv_sem=sig_recv.at[c],
            device_id=(jnp.minimum(me + 1, last), chan), device_id_type=MESH,
        )

    def conv_copy(c):
        return pltpu.make_async_remote_copy(
            src_ref=gwin.at[c, pl.ds(rows, rows), :],
            dst_ref=gwin.at[c, pl.ds(0, rows), :],
            send_sem=gc_send.at[c], recv_sem=gc_recv.at[c],
            device_id=(jnp.maximum(me - 1, 0), chan), device_id_type=MESH,
        )

    loads[0].wait()
    loads[1].wait()

    @pl.loop(0, nb)
    def _(c):
        key = k_ref[:, lanes(c)].astype(f32)
        win[c, rows:, :] = (key * v_ref[:, lanes(c)].astype(f32)).astype(bf16)

        @pl.when(me == 0)
        def _():
            win[c, :rows, :] = jnp.zeros((rows, LANES), bf16)

        @pl.when(me == last)
        def _():
            gwin[c, :rows, :] = jnp.zeros((rows, LANES), bf16)

    pl.semaphore_wait(barrier, n_chan - 1 + len(near))

    @pl.when(me < last)
    def _():
        @pl.loop(0, nb)
        def _(c):
            signal_copy(c).start()

    row, col = iota((rows, rows), 0), iota((rows, rows), 1)
    loads[2].wait()
    taps_b = f_ref[...].astype(bf16)
    negate = (lax.rem(row + col, rows) == 0).astype(f32).astype(bf16)
    frev[...] = jnp.dot(taps_b, negate, preferred_element_type=f32)

    @pl.loop(0, groups, unroll=8)
    def _(g):
        at = pl.ds(pl.multiple_of(g * rows, rows), rows)
        turned = jnp.broadcast_to(frev[pl.ds(g, 1), :], (rows, rows))
        turned = pltpu.roll(turned, 0, 1, stride=1, stride_axis=0)
        fwd[at, :rows] = jnp.where(col > row, turned, 0.0).astype(bf16)
        fwd[at, rows:] = jnp.where(col <= row, turned, 0.0).astype(bf16)

    lane_group = iota((rows, LANES), 1) // members
    flip = (row + col == rows - 1).astype(f32).astype(bf16)
    power[...] = jnp.zeros_like(power)
    inner[...] = jnp.zeros_like(inner)
    for load in loads[3:]:
        load.wait()

    def filtered(window, c):
        total = jnp.zeros((rows, LANES), f32)
        for k in range(per):
            at = pl.ds(pl.multiple_of((c * per + k) * rows, rows), rows)
            out = jnp.dot(fwd[at, :], window, preferred_element_type=f32)
            total = jnp.where(lane_group == k, out, total)
        return total

    @pl.loop(0, nb)
    def _(c):
        @pl.when(me > 0)
        def _():
            signal_copy(c).wait_recv()

        window = win[c]
        mix = filtered(window, c)
        mixed[c] = mix
        lifted = q_ref[:, lanes(c)].astype(f32) * mix
        scaled = gain_ref[:, lanes(c)] * ct_ref[:, lanes(c)].astype(f32)
        square, cross = lifted * lifted, scaled * lifted
        half = LANES // 2
        power[...] += square[:, :half] + square[:, half:]
        inner[...] += cross[:, :half] + cross[:, half:]
        srev[c, :rows, :] = jnp.dot(flip, window[rows:], preferred_element_type=f32).astype(bf16)
        srev[c, rows:, :] = jnp.dot(flip, window[:rows], preferred_element_type=f32).astype(bf16)

    stats[chan, 0:1, :] = jnp.sum(power[...].T, axis=0, keepdims=True)
    stats[chan, 1:2, :] = jnp.sum(inner[...].T, axis=0, keepdims=True)
    stats[chan, 2:, :] = jnp.zeros((6, rows), f32)

    def stat_copy(d, slot):
        return pltpu.make_async_remote_copy(
            src_ref=stats.at[slot], dst_ref=stats.at[slot],
            send_sem=st_send.at[d], recv_sem=st_recv.at[d],
            device_id=(me, chan_peers[d]), device_id_type=MESH,
        )

    for d in range(n_chan - 1):
        stat_copy(d, chan).start()
    for d in range(n_chan - 1):
        stat_copy(d, lax.rem(chan + n_chan - d - 1, n_chan)).wait_recv()
    sums = jnp.sum(stats[...], axis=0)
    recip_row = lax.rsqrt(sums[0:1] / D + 1e-06)
    slope_row = recip_row * recip_row * recip_row * sums[1:2] / D
    recip = jnp.broadcast_to(recip_row, (rows, rows)).T
    slope = jnp.broadcast_to(slope_row, (rows, rows)).T
    power[...] = recip
    inner[...] = slope

    @pl.loop(0, nb)
    def _(c):
        recip = jnp.concatenate([power[...]] * (LANES // rows), axis=1)
        slope = jnp.concatenate([inner[...]] * (LANES // rows), axis=1)
        mix = mixed[c]
        query = q_ref[:, lanes(c)].astype(f32)
        gain = gain_ref[:, lanes(c)]
        lifted = query * mix
        scaled = gain * ct_ref[:, lanes(c)].astype(f32)
        grad_mix = recip * scaled - lifted * slope
        conv = (grad_mix * query).astype(bf16)
        own[c] = conv
        gwin[c, rows:, :] = jnp.dot(flip, conv, preferred_element_type=f32).astype(bf16)

        @pl.when(me > 0)
        def _():
            conv_copy(c).start()

        normed_ref[:, lanes(c)] = (lifted * recip * gain).astype(bf16)
        gq_ref[:, lanes(c)] = (grad_mix * mix).astype(bf16)

    saves = [
        pltpu.make_async_copy(src, dst, out_sem.at[n])
        for n, (src, dst) in enumerate(
            [(normed_ref, normed_hbm), (gq_ref, gq_hbm), (gf_ref, gf_hbm)]
        )
    ]
    saves[0].start()
    saves[1].start()

    def key_save(c):
        return pltpu.make_async_copy(
            gk_ref.at[:, lanes(c)], gk_hbm.at[:, lanes(c)], gk_sem.at[c]
        )

    def value_save(c):
        return pltpu.make_async_copy(
            gv_ref.at[:, lanes(c)], gv_hbm.at[:, lanes(c)], gv_sem.at[c]
        )

    def scatter_copy(d):
        peer = ctx_peer(d)
        return pltpu.make_async_remote_copy(
            src_ref=part.at[pl.ds(pl.multiple_of(peer * per, per), per), :],
            dst_ref=land.at[d],
            send_sem=rs_send.at[d], recv_sem=rs_recv.at[d],
            device_id=(peer, chan), device_id_type=MESH,
        )

    def gather_copy(d, owner):
        at = pl.ds(pl.multiple_of(owner * per, per), per)
        return pltpu.make_async_remote_copy(
            src_ref=gf_ref.at[at, :], dst_ref=gf_ref.at[at, :],
            send_sem=ag_send.at[d], recv_sem=ag_recv.at[d],
            device_id=(ctx_peer(d), chan), device_id_type=MESH,
        )

    @pl.loop(0, nb)
    def _(i):
        c = lax.rem(me + 1 + i, nb) if own_sum else i
        conv = own[c].astype(f32)
        turned = srev[c]
        for k in range(per):
            masked = jnp.where(lane_group == k, conv, 0.0).astype(bf16)
            pairs = lax.dot_general(
                masked, turned, (((1,), (1,)), ((), ())), preferred_element_type=f32
            )
            both = jnp.where(row + col >= rows - 1, pairs[:, :rows], pairs[:, rows:])
            both = pltpu.roll(both, 1, 1, stride=1, stride_axis=0)
            part[pl.ds(c * per + k, 1), :] = jnp.sum(both, axis=0, keepdims=True)
        if own_sum:
            @pl.when(i < nb - 1)
            def _():
                scatter_copy(i).start()

    def back(c):
        @pl.when(me < last)
        def _():
            conv_copy(c).wait_recv()

        turned = filtered(gwin[c], c)
        high = turned.astype(bf16)
        low = (turned - high.astype(f32)).astype(bf16)
        grad_signal = jnp.dot(
            jnp.concatenate([flip, flip], axis=1),
            jnp.concatenate([high, low], axis=0),
            preferred_element_type=f32,
        )
        gk_ref[:, lanes(c)] = (grad_signal * v_ref[:, lanes(c)].astype(f32)).astype(bf16)
        gv_ref[:, lanes(c)] = (grad_signal * k_ref[:, lanes(c)].astype(f32)).astype(bf16)
        key_save(c).start()
        value_save(c).start()

    pl.loop(0, nb // 2)(back)
    if own_sum:
        for d in range(n_ctx - 1):
            scatter_copy(d).wait_recv()
        at = pl.ds(pl.multiple_of(me * per, per), per)
        gf_ref[at, :] = part[at, :] + jnp.sum(land[...], axis=0)
        for d in range(n_ctx - 1):
            gather_copy(d, me).start()
    else:
        gf_ref[...] = part[...]
    pl.loop(nb // 2, nb)(back)

    if own_sum:
        for d in range(n_ctx - 1):
            gather_copy(d, lax.rem(me + n_ctx - d - 1, n_ctx)).wait_recv()
        saves[2].start()
        for d in range(n_ctx - 1):
            gather_copy(d, me).wait_send()
            scatter_copy(d).wait_send()
    else:
        saves[2].start()
    for d in range(n_chan - 1):
        stat_copy(d, chan).wait_send()

    @pl.loop(0, nb)
    def _(c):
        @pl.when(me < last)
        def _():
            signal_copy(c).wait_send()

        @pl.when(me > 0)
        def _():
            conv_copy(c).wait_send()

        key_save(c).wait()
        value_save(c).wait()

    for save in saves:
        save.wait()


def store(*refs):
    held, taken, given = refs[10:15], refs[15], refs[16]
    reads = [pltpu.make_async_copy(refs[n], held[n], taken.at[n]) for n in range(5)]
    writes = [pltpu.make_async_copy(held[n], refs[5 + n], given.at[n]) for n in range(5)]
    for copy in reads:
        copy.start()
    for read, write in zip(reads, writes):
        read.wait()
        write.start()
    for copy in writes:
        copy.wait()


def body(n_ctx, n_chan, query, key_in, value_in, cotangent, filters, norm_gain):
    batch, rows, width = query.shape
    groups, taps = filters.shape
    assert batch == 1 and rows == taps
    members = width // groups
    nb = width // LANES
    own_sum = nb == n_ctx
    f32, bf16 = jnp.float32, jnp.bfloat16
    flat = jax.ShapeDtypeStruct((rows, width), bf16)
    hbm = pl.BlockSpec(memory_space=pltpu.HBM)
    dma = pltpu.SemaphoreType.DMA
    outs = pl.pallas_call(
        functools.partial(kernel, n_ctx, n_chan, members, own_sum),
        out_shape=(flat, flat, flat, flat, jax.ShapeDtypeStruct((groups, taps), f32)),
        in_specs=[hbm] * 6,
        out_specs=(hbm,) * 5,
        scratch_shapes=[
            *[pltpu.VMEM((rows, width), bf16)] * 4,
            pltpu.VMEM((groups, taps), f32),
            dma((3,)), dma((nb,)), dma((nb,)),
            *[pltpu.VMEM((rows, width), bf16)] * 4,
            pltpu.VMEM((groups, taps), f32),
            pltpu.VMEM((1, width), f32),
            dma((6,)),
            pltpu.VMEM((nb, 2 * rows, LANES), bf16),
            pltpu.VMEM((nb, 2 * rows, LANES), bf16),
            pltpu.VMEM((nb, 2 * rows, LANES), bf16),
            pltpu.VMEM((nb, rows, LANES), bf16),
            pltpu.VMEM((groups * rows, 2 * rows), bf16),
            pltpu.VMEM((groups, taps), f32),
            pltpu.VMEM((nb, rows, LANES), f32),
            pltpu.VMEM((rows, rows), f32),
            pltpu.VMEM((rows, rows), f32),
            pltpu.VMEM((n_chan, 8, rows), f32),
            pltpu.VMEM((groups, taps), f32),
            pltpu.VMEM((n_ctx - 1, LANES // members, taps), f32),
            dma((nb,)), dma((nb,)), dma((nb,)), dma((nb,)),
            dma((n_chan - 1,)), dma((n_chan - 1,)),
            dma((n_ctx - 1,)), dma((n_ctx - 1,)), dma((n_ctx - 1,)), dma((n_ctx - 1,)),
        ],
        compiler_params=pltpu.CompilerParams(
            collective_id=0, has_side_effects=True, vmem_limit_bytes=60 << 20
        ),
    )(
        *(x.reshape(rows, width) for x in (query, key_in, value_in, cotangent)),
        filters,
        norm_gain.reshape(1, width),
    )
    outs = pl.pallas_call(
        store,
        out_shape=tuple(jax.ShapeDtypeStruct(x.shape, x.dtype) for x in outs),
        in_specs=[hbm] * 5,
        out_specs=(hbm,) * 5,
        scratch_shapes=[*[pltpu.VMEM(x.shape, x.dtype) for x in outs], dma((5,)), dma((5,))],
        compiler_params=pltpu.CompilerParams(vmem_limit_bytes=60 << 20),
    )(*outs)
    grad_filters = outs[4] if own_sum else lax.psum(outs[4], "ctx")
    return tuple(x.reshape(1, rows, width) for x in outs[:4]) + (grad_filters,)


def solution(mesh):
    spread = P(None, "ctx", "chan")
    return jax.shard_map(
        functools.partial(body, mesh.shape["ctx"], mesh.shape["chan"]),
        mesh=mesh,
        in_specs=(spread,) * 4 + (P("chan", None), P("chan")),
        out_specs=(spread,) * 4 + (P("chan", None),),
        check_vma=False,
    )
```

```python
import functools

import jax
import jax.numpy as jnp
from jax import lax
from jax.experimental import pallas as pl
from jax.experimental.pallas import tpu as pltpu
from jax.sharding import PartitionSpec as P

D = 8192
LANES = 256
MESH = pl.DeviceIdType.MESH


def iota(shape, axis):
    return lax.broadcasted_iota(jnp.int32, shape, axis)


def kernel(
    n_ctx, n_chan, members, own_sum,
    q_hbm, k_hbm, v_hbm, ct_hbm, f_hbm, gain_hbm,
    normed_hbm, gq_hbm, gk_hbm, gv_hbm, gf_hbm,
    normed_ref, gq_ref, gk_ref, gv_ref, gf_ref, out_sem, gk_sem, gv_sem,
    q_ref, k_ref, v_ref, ct_ref, f_ref, gain_ref, in_sem,
    win, gwin, srev, own, fwd, frev, mixed, power, inner, stats, part, sent, land,
    sig_send, sig_recv, gc_send, gc_recv, st_send, st_recv, rs_send, rs_recv, ag_send, ag_recv,
):
    f32, bf16 = jnp.float32, jnp.bfloat16
    rows = q_ref.shape[0]
    nb = q_ref.shape[1] // LANES
    groups = f_ref.shape[0]
    per = LANES // members
    me, chan = lax.axis_index("ctx"), lax.axis_index("chan")
    last = n_ctx - 1

    loads = [
        pltpu.make_async_copy(src, dst, in_sem.at[n])
        for n, (src, dst) in enumerate([
            (k_hbm, k_ref), (v_hbm, v_ref), (f_hbm, f_ref),
            (q_hbm, q_ref), (ct_hbm, ct_ref), (gain_hbm, gain_ref),
        ])
    ]
    for load in loads:
        load.start()
    barrier = pltpu.get_barrier_semaphore()
    chan_peers = [lax.rem(chan + d, n_chan) for d in range(1, n_chan)]
    near = range(1, n_ctx) if own_sum else sorted({1, n_ctx - 1})
    for peer in chan_peers:
        pl.semaphore_signal(barrier, inc=1, device_id=(me, peer), device_id_type=MESH)
    for d in near:
        pl.semaphore_signal(
            barrier, inc=1, device_id=(lax.rem(me + d, n_ctx), chan), device_id_type=MESH
        )

    def ctx_peer(d):
        return lax.rem(me + d + 1, n_ctx)

    def lanes(c):
        return pl.ds(pl.multiple_of(c * LANES, LANES), LANES)

    def signal_copy(c):
        return pltpu.make_async_remote_copy(
            src_ref=win.at[c, pl.ds(rows, rows), :],
            dst_ref=win.at[c, pl.ds(0, rows), :],
            send_sem=sig_send.at[c], recv_sem=sig_recv.at[c],
            device_id=(jnp.minimum(me + 1, last), chan), device_id_type=MESH,
        )

    def conv_copy(c):
        return pltpu.make_async_remote_copy(
            src_ref=gwin.at[c, pl.ds(rows, rows), :],
            dst_ref=gwin.at[c, pl.ds(0, rows), :],
            send_sem=gc_send.at[c], recv_sem=gc_recv.at[c],
            device_id=(jnp.maximum(me - 1, 0), chan), device_id_type=MESH,
        )

    loads[0].wait()
    loads[1].wait()

    @pl.loop(0, nb)
    def _(c):
        key = k_ref[:, lanes(c)].astype(f32)
        win[c, rows:, :] = (key * v_ref[:, lanes(c)].astype(f32)).astype(bf16)

        @pl.when(me == 0)
        def _():
            win[c, :rows, :] = jnp.zeros((rows, LANES), bf16)

        @pl.when(me == last)
        def _():
            gwin[c, :rows, :] = jnp.zeros((rows, LANES), bf16)

    pl.semaphore_wait(barrier, n_chan - 1 + len(near))

    @pl.when(me < last)
    def _():
        @pl.loop(0, nb)
        def _(c):
            signal_copy(c).start()

    row, col = iota((rows, rows), 0), iota((rows, rows), 1)
    loads[2].wait()
    taps_b = f_ref[...].astype(bf16)
    negate = (lax.rem(row + col, rows) == 0).astype(f32).astype(bf16)
    frev[...] = jnp.dot(taps_b, negate, preferred_element_type=f32)

    @pl.loop(0, groups, unroll=8)
    def _(g):
        at = pl.ds(pl.multiple_of(g * rows, rows), rows)
        turned = jnp.broadcast_to(frev[pl.ds(g, 1), :], (rows, rows))
        turned = pltpu.roll(turned, 0, 1, stride=1, stride_axis=0)
        fwd[at, :rows] = jnp.where(col > row, turned, 0.0).astype(bf16)
        fwd[at, rows:] = jnp.where(col <= row, turned, 0.0).astype(bf16)

    lane_group = iota((rows, LANES), 1) // members
    flip = (row + col == rows - 1).astype(f32).astype(bf16)
    power[...] = jnp.zeros_like(power)
    inner[...] = jnp.zeros_like(inner)
    for load in loads[3:]:
        load.wait()

    def filtered(window, c):
        total = jnp.zeros((rows, LANES), f32)
        for k in range(per):
            at = pl.ds(pl.multiple_of((c * per + k) * rows, rows), rows)
            out = jnp.dot(fwd[at, :], window, preferred_element_type=f32)
            total = jnp.where(lane_group == k, out, total)
        return total

    @pl.loop(0, nb)
    def _(c):
        @pl.when(me > 0)
        def _():
            signal_copy(c).wait_recv()

        window = win[c]
        mix = filtered(window, c)
        mixed[c] = mix
        lifted = q_ref[:, lanes(c)].astype(f32) * mix
        scaled = gain_ref[:, lanes(c)] * ct_ref[:, lanes(c)].astype(f32)
        square, cross = lifted * lifted, scaled * lifted
        half = LANES // 2
        power[...] += square[:, :half] + square[:, half:]
        inner[...] += cross[:, :half] + cross[:, half:]
        srev[c, :rows, :] = jnp.dot(flip, window[rows:], preferred_element_type=f32).astype(bf16)
        srev[c, rows:, :] = jnp.dot(flip, window[:rows], preferred_element_type=f32).astype(bf16)

    stats[chan, 0:1, :] = jnp.sum(power[...].T, axis=0, keepdims=True)
    stats[chan, 1:2, :] = jnp.sum(inner[...].T, axis=0, keepdims=True)
    stats[chan, 2:, :] = jnp.zeros((6, rows), f32)

    def stat_copy(d, slot):
        return pltpu.make_async_remote_copy(
            src_ref=stats.at[slot], dst_ref=stats.at[slot],
            send_sem=st_send.at[d], recv_sem=st_recv.at[d],
            device_id=(me, chan_peers[d]), device_id_type=MESH,
        )

    for d in range(n_chan - 1):
        stat_copy(d, chan).start()
    for d in range(n_chan - 1):
        stat_copy(d, lax.rem(chan + n_chan - d - 1, n_chan)).wait_recv()
    sums = jnp.sum(stats[...], axis=0)
    recip_row = lax.rsqrt(sums[0:1] / D + 1e-06)
    slope_row = recip_row * recip_row * recip_row * sums[1:2] / D
    recip = jnp.broadcast_to(recip_row, (rows, rows)).T
    slope = jnp.broadcast_to(slope_row, (rows, rows)).T
    power[...] = recip
    inner[...] = slope

    @pl.loop(0, nb)
    def _(c):
        recip = jnp.concatenate([power[...]] * (LANES // rows), axis=1)
        slope = jnp.concatenate([inner[...]] * (LANES // rows), axis=1)
        mix = mixed[c]
        query = q_ref[:, lanes(c)].astype(f32)
        gain = gain_ref[:, lanes(c)]
        lifted = query * mix
        scaled = gain * ct_ref[:, lanes(c)].astype(f32)
        grad_mix = recip * scaled - lifted * slope
        conv = (grad_mix * query).astype(bf16)
        own[c] = conv
        gwin[c, rows:, :] = jnp.dot(flip, conv, preferred_element_type=f32).astype(bf16)

        @pl.when(me > 0)
        def _():
            conv_copy(c).start()

        normed_ref[:, lanes(c)] = (lifted * recip * gain).astype(bf16)
        gq_ref[:, lanes(c)] = (grad_mix * mix).astype(bf16)

    saves = [
        pltpu.make_async_copy(src, dst, out_sem.at[n])
        for n, (src, dst) in enumerate(
            [(normed_ref, normed_hbm), (gq_ref, gq_hbm), (gf_ref, gf_hbm)]
        )
    ]
    saves[0].start()
    saves[1].start()

    def key_save(c):
        return pltpu.make_async_copy(
            gk_ref.at[:, lanes(c)], gk_hbm.at[:, lanes(c)], gk_sem.at[c]
        )

    def value_save(c):
        return pltpu.make_async_copy(
            gv_ref.at[:, lanes(c)], gv_hbm.at[:, lanes(c)], gv_sem.at[c]
        )

    def scatter_copy(d):
        peer = ctx_peer(d)
        return pltpu.make_async_remote_copy(
            src_ref=sent.at[pl.ds(pl.multiple_of(peer * per, per), per), :],
            dst_ref=land.at[d],
            send_sem=rs_send.at[d], recv_sem=rs_recv.at[d],
            device_id=(peer, chan), device_id_type=MESH,
        )

    def gather_copy(d, owner):
        at = pl.ds(pl.multiple_of(owner * per, per), per)
        return pltpu.make_async_remote_copy(
            src_ref=gf_ref.at[at, :], dst_ref=gf_ref.at[at, :],
            send_sem=ag_send.at[d], recv_sem=ag_recv.at[d],
            device_id=(ctx_peer(d), chan), device_id_type=MESH,
        )

    @pl.loop(0, nb)
    def _(i):
        c = lax.rem(me + 1 + i, nb) if own_sum else i
        conv = own[c].astype(f32)
        turned = srev[c]
        for k in range(per):
            masked = jnp.where(lane_group == k, conv, 0.0).astype(bf16)
            pairs = lax.dot_general(
                masked, turned, (((1,), (1,)), ((), ())), preferred_element_type=f32
            )
            both = jnp.where(row + col >= rows - 1, pairs[:, :rows], pairs[:, rows:])
            both = pltpu.roll(both, 1, 1, stride=1, stride_axis=0)
            part[pl.ds(c * per + k, 1), :] = jnp.sum(both, axis=0, keepdims=True)
        if own_sum:
            at = pl.ds(pl.multiple_of(c * per, per), per)
            sent[at, :] = part[at, :].astype(bf16)
        if own_sum:
            @pl.when(i < nb - 1)
            def _():
                scatter_copy(i).start()

    def back(c):
        @pl.when(me < last)
        def _():
            conv_copy(c).wait_recv()

        turned = filtered(gwin[c], c)
        high = turned.astype(bf16)
        low = (turned - high.astype(f32)).astype(bf16)
        grad_signal = jnp.dot(
            jnp.concatenate([flip, flip], axis=1),
            jnp.concatenate([high, low], axis=0),
            preferred_element_type=f32,
        )
        gk_ref[:, lanes(c)] = (grad_signal * v_ref[:, lanes(c)].astype(f32)).astype(bf16)
        gv_ref[:, lanes(c)] = (grad_signal * k_ref[:, lanes(c)].astype(f32)).astype(bf16)
        key_save(c).start()
        value_save(c).start()

    pl.loop(0, nb // 2)(back)
    if own_sum:
        for d in range(n_ctx - 1):
            scatter_copy(d).wait_recv()
        at = pl.ds(pl.multiple_of(me * per, per), per)
        gf_ref[at, :] = part[at, :] + jnp.sum(land[...].astype(f32), axis=0)
        for d in range(n_ctx - 1):
            gather_copy(d, me).start()
    else:
        gf_ref[...] = part[...]
    pl.loop(nb // 2, nb)(back)

    if own_sum:
        for d in range(n_ctx - 1):
            gather_copy(d, lax.rem(me + n_ctx - d - 1, n_ctx)).wait_recv()
        saves[2].start()
        for d in range(n_ctx - 1):
            gather_copy(d, me).wait_send()
            scatter_copy(d).wait_send()
    else:
        saves[2].start()
    for d in range(n_chan - 1):
        stat_copy(d, chan).wait_send()

    @pl.loop(0, nb)
    def _(c):
        @pl.when(me < last)
        def _():
            signal_copy(c).wait_send()

        @pl.when(me > 0)
        def _():
            conv_copy(c).wait_send()

        key_save(c).wait()
        value_save(c).wait()

    for save in saves:
        save.wait()


def store(*refs):
    held, taken, given = refs[10:15], refs[15], refs[16]
    reads = [pltpu.make_async_copy(refs[n], held[n], taken.at[n]) for n in range(5)]
    writes = [pltpu.make_async_copy(held[n], refs[5 + n], given.at[n]) for n in range(5)]
    for copy in reads:
        copy.start()
    for read, write in zip(reads, writes):
        read.wait()
        write.start()
    for copy in writes:
        copy.wait()


def body(n_ctx, n_chan, query, key_in, value_in, cotangent, filters, norm_gain):
    batch, rows, width = query.shape
    groups, taps = filters.shape
    assert batch == 1 and rows == taps
    members = width // groups
    nb = width // LANES
    own_sum = nb == n_ctx
    f32, bf16 = jnp.float32, jnp.bfloat16
    flat = jax.ShapeDtypeStruct((rows, width), bf16)
    hbm = pl.BlockSpec(memory_space=pltpu.HBM)
    dma = pltpu.SemaphoreType.DMA
    outs = pl.pallas_call(
        functools.partial(kernel, n_ctx, n_chan, members, own_sum),
        out_shape=(flat, flat, flat, flat, jax.ShapeDtypeStruct((groups, taps), f32)),
        in_specs=[hbm] * 6,
        out_specs=(hbm,) * 5,
        scratch_shapes=[
            *[pltpu.VMEM((rows, width), bf16)] * 4,
            pltpu.VMEM((groups, taps), f32),
            dma((3,)), dma((nb,)), dma((nb,)),
            *[pltpu.VMEM((rows, width), bf16)] * 4,
            pltpu.VMEM((groups, taps), f32),
            pltpu.VMEM((1, width), f32),
            dma((6,)),
            pltpu.VMEM((nb, 2 * rows, LANES), bf16),
            pltpu.VMEM((nb, 2 * rows, LANES), bf16),
            pltpu.VMEM((nb, 2 * rows, LANES), bf16),
            pltpu.VMEM((nb, rows, LANES), bf16),
            pltpu.VMEM((groups * rows, 2 * rows), bf16),
            pltpu.VMEM((groups, taps), f32),
            pltpu.VMEM((nb, rows, LANES), f32),
            pltpu.VMEM((rows, rows), f32),
            pltpu.VMEM((rows, rows), f32),
            pltpu.VMEM((n_chan, 8, rows), f32),
            pltpu.VMEM((groups, taps), f32),
            pltpu.VMEM((groups, taps), bf16),
            pltpu.VMEM((n_ctx - 1, LANES // members, taps), bf16),
            dma((nb,)), dma((nb,)), dma((nb,)), dma((nb,)),
            dma((n_chan - 1,)), dma((n_chan - 1,)),
            dma((n_ctx - 1,)), dma((n_ctx - 1,)), dma((n_ctx - 1,)), dma((n_ctx - 1,)),
        ],
        compiler_params=pltpu.CompilerParams(
            collective_id=0, has_side_effects=True, vmem_limit_bytes=60 << 20
        ),
    )(
        *(x.reshape(rows, width) for x in (query, key_in, value_in, cotangent)),
        filters,
        norm_gain.reshape(1, width),
    )
    outs = pl.pallas_call(
        store,
        out_shape=tuple(jax.ShapeDtypeStruct(x.shape, x.dtype) for x in outs),
        in_specs=[hbm] * 5,
        out_specs=(hbm,) * 5,
        scratch_shapes=[*[pltpu.VMEM(x.shape, x.dtype) for x in outs], dma((5,)), dma((5,))],
        compiler_params=pltpu.CompilerParams(vmem_limit_bytes=60 << 20),
    )(*outs)
    grad_filters = outs[4] if own_sum else lax.psum(outs[4], "ctx")
    return tuple(x.reshape(1, rows, width) for x in outs[:4]) + (grad_filters,)


def solution(mesh):
    spread = P(None, "ctx", "chan")
    return jax.shard_map(
        functools.partial(body, mesh.shape["ctx"], mesh.shape["chan"]),
        mesh=mesh,
        in_specs=(spread,) * 4 + (P("chan", None), P("chan")),
        out_specs=(spread,) * 4 + (P("chan", None),),
        check_vma=False,
    )
```
